32 devices in a mesh: dp: 4 (over z), row: 2 (over x), col: 4 (over y, core).
Axes of the slice: x: 2, y: 2, z: 4, core: 2. Of those that a mesh axis runs over, the one named last changes fastest.
Arguments:
- inputs: bfloat16 [4, 192, 16, 512], P('dp', None, 'row', 'col'), may hold values from -16 to 16
- norm_gain: float32 [192], replicated, may hold values from 0.25 to 1.75
- w_expand: bfloat16 [192, 768], replicated, may hold values from -0.4375 to 0.4375
- kernel: float32 [768, 9], replicated, may hold values from -2 to 2
- w_squeeze: float32 [768, 48], replicated, may hold values from -1.5 to 1.5
- w_excite: float32 [48, 768], replicated, may hold values from -6 to 6
- w_project: bfloat16 [768, 192], replicated, may hold values from -0.21875 to 0.21875
- cotangent: bfloat16 [4, 192, 16, 512], P('dp', None, 'row', 'col'), may hold values from -16 to 16
Outputs:
- output: bfloat16 [4, 192, 16, 512], P('dp', None, 'row', 'col')
- grad_inputs: bfloat16 [4, 192, 16, 512], P('dp', None, 'row', 'col')
- grad_gain: float32 [192], replicated
- grad_w_expand: float32 [192, 768], replicated
- grad_kernel: float32 [768, 9], replicated
- grad_w_squeeze: float32 [768, 48], replicated
- grad_w_excite: float32 [48, 768], replicated
- grad_w_project: float32 [768, 192], replicated
The draws below stay inside these ranges and needn't reach their ends.
All inputs are finite; a program needn't handle non-finite values.
Results may differ from the reference program's by a relative error of at most 0.0019.
Values may be sent and summed in bfloat16 or wider, within the bound.
A program may use at most 64 MiB of HBM per device.

```python
import jax
import jax.numpy as jnp
from jax import lax

C = 192
E = 768
S = 48
SAMPLES = 4
NH = 16
NW = 512


def draw_inputs(key, part):
    keys = jax.random.split(key, 4)
    noise = jax.random.normal(keys[0], (SAMPLES, C, NH, NW), jnp.float32)
    lean = jax.random.normal(keys[3], (SAMPLES, C, 1, 1), jnp.float32)
    chan = jnp.exp(jax.random.uniform(keys[1], (1, C, 1, 1), jnp.float32, -1.15, 1.15))
    cell = jnp.exp(jax.random.uniform(keys[2], (SAMPLES, 1, NH, NW), jnp.float32, -1.15, 1.15))
    down = lax.broadcasted_iota(jnp.float32, (1, 1, NH, NW), 2) / NH
    across = lax.broadcasted_iota(jnp.float32, (1, 1, NH, NW), 3) / NW
    ramp = 0.3 + 0.9 * (down + across)
    return jnp.clip(noise * chan * cell + lean * ramp, -16.0, 16.0).astype(jnp.bfloat16)


def draw_cotangent(key, part):
    keys = jax.random.split(key, 3)
    noise = jax.random.normal(keys[0], (SAMPLES, C, NH, NW), jnp.float32)
    lean = jax.random.normal(keys[1], (SAMPLES, C, 1, 1), jnp.float32)
    cell = jnp.exp(jax.random.uniform(keys[2], (SAMPLES, 1, NH, NW), jnp.float32, -0.7, 0.7))
    return jnp.clip(noise * cell + lean, -16.0, 16.0).astype(jnp.bfloat16)


def gaussian(rng, extent, scale, reach, held_as=jnp.bfloat16):
    return jnp.clip(scale * jax.random.normal(rng, extent, jnp.float32), -reach, reach).astype(held_as)


def setup_inputs(seed: int = 0) -> dict:
    seeds = jax.random.split(jax.random.key(seed), 9)
    inputs = draw_inputs(jax.random.fold_in(seeds[8], 71), 0)
    norm_gain = jnp.clip(1.0 + 0.15 * jax.random.normal(seeds[1], (C,), jnp.float32), 0.25, 1.75)
    w_expand = gaussian(seeds[2], (C, E), C ** -0.5, 0.4375)
    kernel = gaussian(seeds[3], (E, 9), 9 ** -0.5, 2.0, jnp.float32)
    w_squeeze = gaussian(seeds[4], (E, S), (3 * E ** -0.5), 1.5, jnp.float32)
    w_excite = gaussian(seeds[5], (S, E), (4 * S ** -0.5), 6.0, jnp.float32)
    w_project = gaussian(seeds[6], (E, C), E ** -0.5, 0.21875)
    cotangent = draw_cotangent(jax.random.fold_in(seeds[8], 71), 0)
    return {"inputs": inputs, "norm_gain": norm_gain, "w_expand": w_expand, "kernel": kernel, "w_squeeze": w_squeeze, "w_excite": w_excite, "w_project": w_project, "cotangent": cotangent}


EPS = 1e-06
HIGH = lax.Precision.HIGHEST

def silu_slope(value):
    sig = jax.nn.sigmoid(value)
    return sig * (1.0 + value * (1.0 - sig))

def one_sample(inputs, cotangent, norm_gain, w_expand, kernel, w_squeeze, w_excite, w_project):
    chans, height, width = inputs.shape
    widened = inputs.astype(jnp.float32)
    inverse = lax.rsqrt(lax.optimization_barrier(jnp.mean(widened * widened, axis=0, keepdims=True)) + EPS)
    normed = widened * inverse
    scaled = (normed * norm_gain[:, None, None]).astype(jnp.bfloat16)
    pre = jnp.einsum('chw,ce->ehw', scaled.astype(jnp.float32), w_expand.astype(jnp.float32), precision=HIGH)
    hidden = jax.nn.silu(pre).astype(jnp.bfloat16)
    padded = jnp.pad(hidden, ((0, 0), (1, 1), (1, 1))).astype(jnp.float32)
    conv = jnp.zeros(pre.shape, jnp.float32)
    for tap in range(9):
        drow, dcol = (tap // 3, tap % 3)
        conv = conv + kernel[:, tap][:, None, None] * padded[:, drow:drow + height, dcol:dcol + width]
    act = jax.nn.silu(conv)
    pooled = lax.optimization_barrier(jnp.mean(act, axis=(1, 2)))
    squeeze_pre = jnp.dot(pooled, w_squeeze, precision=HIGH)
    squeezed = jax.nn.silu(squeeze_pre)
    excite_pre = jnp.dot(squeezed, w_excite, precision=HIGH)
    excite = jax.nn.sigmoid(excite_pre)
    gated = (act * excite[:, None, None]).astype(jnp.bfloat16)
    proj = jnp.einsum('ehw,ec->chw', gated.astype(jnp.float32), w_project.astype(jnp.float32), precision=HIGH)
    output = (widened + proj).astype(jnp.bfloat16)
    cot = cotangent.astype(jnp.float32)
    grad_gated = jnp.einsum('chw,ec->ehw', cot, w_project.astype(jnp.float32), precision=HIGH)
    grad_project = jnp.einsum('ehw,chw->ec', gated.astype(jnp.float32), cot, precision=HIGH)
    grad_excite = lax.optimization_barrier(jnp.sum(grad_gated * act, axis=(1, 2)))
    grad_epre = grad_excite * excite * (1.0 - excite)
    grad_wexc = squeezed[:, None] * grad_epre[None, :]
    grad_spre = jnp.dot(w_excite, grad_epre, precision=HIGH) * silu_slope(squeeze_pre)
    grad_wsq = pooled[:, None] * grad_spre[None, :]
    grad_pooled = jnp.dot(w_squeeze, grad_spre, precision=HIGH)
    grad_act = grad_gated * excite[:, None, None] + (grad_pooled / (height * width))[:, None, None]
    grad_conv = (grad_act * silu_slope(conv)).astype(jnp.bfloat16)
    grad_pad = jnp.pad(grad_conv, ((0, 0), (1, 1), (1, 1))).astype(jnp.float32)
    grad_hidden = jnp.zeros(pre.shape, jnp.float32)
    taps = []
    for tap in range(9):
        drow, dcol = (tap // 3, tap % 3)
        grad_hidden = grad_hidden + kernel[:, tap][:, None, None] * grad_pad[:, 2 - drow:2 - drow + height, 2 - dcol:2 - dcol + width]
        taps.append(lax.optimization_barrier(jnp.sum(grad_conv.astype(jnp.float32) * padded[:, drow:drow + height, dcol:dcol + width], axis=(1, 2))))
    grad_kernel = jnp.stack(taps, axis=1)
    grad_pre = (grad_hidden * silu_slope(pre)).astype(jnp.bfloat16)
    grad_wexp = jnp.einsum('chw,ehw->ce', scaled.astype(jnp.float32), grad_pre.astype(jnp.float32), precision=HIGH)
    grad_scaled = jnp.einsum('ce,ehw->chw', w_expand.astype(jnp.float32), grad_pre.astype(jnp.float32), precision=HIGH)
    grad_gain = lax.optimization_barrier(jnp.sum(grad_scaled * normed, axis=(1, 2)))
    grad_normed = grad_scaled * norm_gain[:, None, None]
    grad_in = inverse * (grad_normed - normed * lax.optimization_barrier(jnp.mean(grad_normed * normed, axis=0, keepdims=True))) + cot
    return (output, grad_in.astype(jnp.bfloat16), grad_gain, grad_wexp, grad_kernel, grad_wsq, grad_wexc, grad_project)

def reference(inputs, norm_gain, w_expand, kernel, w_squeeze, w_excite, w_project, cotangent):

    def step(pair):
        return one_sample(pair[0], pair[1], norm_gain, w_expand, kernel, w_squeeze, w_excite, w_project)
    result = lax.map(step, (inputs, cotangent))
    return (result[0], result[1], lax.optimization_barrier(jnp.sum(result[2], axis=0)), lax.optimization_barrier(jnp.sum(result[3], axis=0)), lax.optimization_barrier(jnp.sum(result[4], axis=0)), lax.optimization_barrier(jnp.sum(result[5], axis=0)), lax.optimization_barrier(jnp.sum(result[6], axis=0)), lax.optimization_barrier(jnp.sum(result[7], axis=0)))
```

```python
import jax
import jax.numpy as jnp
from jax import lax
from jax.experimental import pallas as pl
from jax.experimental.pallas import tpu as pltpu
from jax.sharding import PartitionSpec as P

EPS = 1e-06
HIGH = lax.Precision.HIGHEST

MESH = pl.DeviceIdType.MESH

def sum_kernel(v_ref, out_ref, mate_buf, acc1, group_buf, acc2, deep_buf, send, recv):
    groups, deep = v_ref.shape[1], v_ref.shape[2]
    half_cols = lax.axis_size("col") // 2
    d, w, c = (lax.axis_index(a) for a in ("dp", "row", "col"))
    core = lax.rem(c, 2)
    g = w * half_cols + c // 2

    def mate():
        return (d, w, c + 1 - 2 * core)

    def peer(s):
        at = lax.rem(g + s, groups)
        return at, (d, at // half_cols, lax.rem(at, half_cols) * 2 + core)

    def layer(s):
        at = lax.rem(d + s, deep)
        return at, (at, w, c)

    barrier = pltpu.get_barrier_semaphore()
    others = [mate()] + [peer(s)[1] for s in range(1, groups)]
    others += [layer(s)[1] for s in range(1, deep)]
    for other in others:
        pl.semaphore_signal(barrier, inc=1, device_id=other, device_id_type=MESH)
    pl.semaphore_wait(barrier, len(others))

    def copy(src, dst, n, to):
        return pltpu.make_async_remote_copy(
            src_ref=src,
            dst_ref=dst,
            send_sem=send.at[n],
            recv_sem=recv.at[n],
            device_id=to,
            device_id_type=MESH,
        )

    def run(copies):
        for one in copies:
            one.start()
        for one in copies:
            one.wait()

    run([copy(v_ref.at[1 - core], mate_buf, 0, mate())])
    acc1[...] = v_ref[core] + mate_buf[...]
    n = 0
    moves = []
    for s in range(1, groups):
        at, to = peer(s)
        moves.append(copy(acc1.at[at], group_buf.at[s - 1], n + s, to))
    run(moves)
    part = acc1[g]
    for s in range(1, groups):
        part = part + group_buf[s - 1]
    acc2[...] = part
    n += groups - 1
    moves = []
    for s in range(1, deep):
        at, to = layer(s)
        moves.append(copy(acc2.at[at], deep_buf.at[s - 1], n + s, to))
    run(moves)
    part = acc2[d]
    for s in range(1, deep):
        part = part + deep_buf[s - 1]
    out_ref[core, g, d] = part
    n += deep - 1
    mine = out_ref.at[core, g, d]
    run([copy(mine, mine, n + s, layer(s)[1]) for s in range(1, deep)])
    n += deep - 1
    mine = out_ref.at[core, g]
    run([copy(mine, mine, n + s, peer(s)[1]) for s in range(1, groups)])
    n += groups
    mine = out_ref.at[core]
    run([copy(mine, mine, n, mate())])


def sum_all(values):
    rows, cols = values.shape
    groups = lax.axis_size("row") * (lax.axis_size("col") // 2)
    deep = lax.axis_size("dp")
    each = -(-rows // (2 * groups * deep))
    wide = -(-cols // 128) * 128
    full = 2 * groups * deep * each
    laid = jnp.pad(values, ((0, full - rows), (0, wide - cols)))
    laid = laid.reshape(2, groups, deep, each, wide)
    f32 = jnp.float32
    count = 2 * (1 + groups - 1 + deep - 1) + 1
    total = pl.pallas_call(
        sum_kernel,
        out_shape=jax.ShapeDtypeStruct(laid.shape, f32),
        in_specs=[pl.BlockSpec(memory_space=pltpu.VMEM)],
        out_specs=pl.BlockSpec(memory_space=pltpu.VMEM),
        scratch_shapes=[
            pltpu.VMEM((groups, deep, each, wide), f32),
            pltpu.VMEM((groups, deep, each, wide), f32),
            pltpu.VMEM((max(groups - 1, 1), deep, each, wide), f32),
            pltpu.VMEM((deep, each, wide), f32),
            pltpu.VMEM((max(deep - 1, 1), each, wide), f32),
            pltpu.SemaphoreType.DMA((count,)),
            pltpu.SemaphoreType.DMA((count,)),
        ],
        compiler_params=pltpu.CompilerParams(
            collective_id=0, has_side_effects=True, vmem_limit_bytes=48 << 20
        ),
        name="sum_grads",
    )(laid)
    return total.reshape(full, wide)[:rows, :cols]


def with_halo(shard, sides, width):
    for axis, dim in sides:
        count, length = (lax.axis_size(axis), shard.shape[dim])
        up = [(i, (i + 1) % count) for i in range(count - 1)]
        down = [(j, i) for i, j in up]
        last = lax.slice_in_dim(shard, length - width, length, axis=dim)
        leading = lax.slice_in_dim(shard, 0, width, axis=dim)
        before = lax.ppermute(last, axis, up)
        after = lax.ppermute(leading, axis, down)
        shard = jnp.concatenate([before, shard, after], axis=dim)
    return shard


def silu_slope(value):
    sig = jax.nn.sigmoid(value)
    return sig * (1.0 + value * (1.0 - sig))


def normalize(inputs, norm_gain):
    widened = inputs.astype(jnp.float32)
    inverse = lax.rsqrt(jnp.mean(widened * widened, axis=1, keepdims=True) + EPS)
    normed = widened * inverse
    scaled = (normed * norm_gain[None, :, None, None]).astype(jnp.bfloat16)
    return (normed, inverse, scaled)


def expand(scaled, w_expand):
    return jnp.einsum("bchw,ce->behw", scaled, w_expand, preferred_element_type=jnp.float32)


def depthwise(hidden_pad, kernel, out_rows, out_cols):
    total = jnp.zeros((hidden_pad.shape[0], hidden_pad.shape[1], out_rows, out_cols), jnp.float32)
    for tap in range(9):
        drow, dcol = (tap // 3, tap % 3)
        total = (
            total
            + kernel[:, tap][None, :, None, None]
            * hidden_pad[:, :, drow : drow + out_rows, dcol : dcol + out_cols]
        )
    return total


def local(inputs, norm_gain, w_expand, kernel, w_squeeze, w_excite, w_project, cotangent):
    batch, chans, rows, cols = inputs.shape
    pixels = rows * cols * lax.axis_size("row") * lax.axis_size("col")
    normed, inverse, scaled = normalize(inputs, norm_gain)
    pre = expand(scaled, w_expand)
    hidden = jax.nn.silu(pre).astype(jnp.bfloat16)
    hidden_pad = with_halo(hidden, (("row", 2), ("col", 3)), 1)
    conv = depthwise(hidden_pad, kernel, rows, cols)
    act = jax.nn.silu(conv)
    pooled = lax.psum(jnp.sum(act, axis=(2, 3)), ("row", "col")) / pixels
    squeeze_pre = jnp.dot(pooled, w_squeeze, precision=HIGH)
    squeezed = jax.nn.silu(squeeze_pre)
    excite_pre = jnp.dot(squeezed, w_excite, precision=HIGH)
    excite = jax.nn.sigmoid(excite_pre)
    gated = (act * excite[:, :, None, None]).astype(jnp.bfloat16)
    proj = jnp.einsum("behw,ec->bchw", gated, w_project, preferred_element_type=jnp.float32)
    output = (inputs.astype(jnp.float32) + proj).astype(jnp.bfloat16)
    grad_gated = jnp.einsum(
        "bchw,ec->behw", cotangent, w_project, preferred_element_type=jnp.float32
    )
    grad_project = jnp.einsum("behw,bchw->ec", gated, cotangent, preferred_element_type=jnp.float32)
    grad_excite = lax.psum(jnp.sum(grad_gated * act, axis=(2, 3)), ("row", "col"))
    grad_epre = grad_excite * excite * (1.0 - excite)
    grad_wexc = jnp.einsum("bs,be->se", squeezed, grad_epre, precision=HIGH)
    grad_spre = jnp.einsum("be,se->bs", grad_epre, w_excite, precision=HIGH) * silu_slope(
        squeeze_pre
    )
    grad_wsq = jnp.einsum("be,bs->es", pooled, grad_spre, precision=HIGH)
    grad_pooled = jnp.einsum("bs,es->be", grad_spre, w_squeeze, precision=HIGH)
    grad_act = grad_gated * excite[:, :, None, None] + (grad_pooled / pixels)[:, :, None, None]
    grad_conv = (grad_act * silu_slope(conv)).astype(jnp.bfloat16)
    grad_pad = with_halo(grad_conv, (("row", 2), ("col", 3)), 1)
    grad_hidden = jnp.zeros(pre.shape, jnp.float32)
    taps = []
    for tap in range(9):
        drow, dcol = (tap // 3, tap % 3)
        grad_hidden = (
            grad_hidden
            + kernel[:, tap][None, :, None, None]
            * grad_pad[:, :, 2 - drow : 2 - drow + rows, 2 - dcol : 2 - dcol + cols]
        )
        taps.append(
            jnp.sum(
                grad_conv.astype(jnp.float32)
                * hidden_pad[:, :, drow : drow + rows, dcol : dcol + cols].astype(jnp.float32),
                axis=(0, 2, 3),
            )
        )
    grad_kernel = jnp.stack(taps, axis=1)
    grad_pre = (grad_hidden * silu_slope(pre)).astype(jnp.bfloat16)
    grad_wexp = jnp.einsum("bchw,behw->ce", scaled, grad_pre, preferred_element_type=jnp.float32)
    grad_scaled = jnp.einsum(
        "ce,behw->bchw", w_expand, grad_pre, preferred_element_type=jnp.float32
    )
    grad_gain = jnp.sum(grad_scaled * normed, axis=(0, 2, 3))
    grad_normed = grad_scaled * norm_gain[None, :, None, None]
    grad_in = inverse * (
        grad_normed - normed * jnp.mean(grad_normed * normed, axis=1, keepdims=True)
    ) + cotangent.astype(jnp.float32)
    lead = jnp.logical_and(lax.axis_index("row") == 0, lax.axis_index("col") == 0)
    keep = lead.astype(jnp.float32)
    hidden_n = grad_project.shape[0]
    pieces = [
        grad_project,
        grad_wexp.T,
        grad_kernel,
        grad_wsq * keep,
        grad_wexc.T * keep,
        jnp.pad(grad_gain, (0, hidden_n - chans))[:, None],
    ]
    sizes = [p.shape[1] for p in pieces]
    total = sum_all(jnp.concatenate(pieces, axis=1))
    ends = [sum(sizes[: n + 1]) for n in range(len(sizes))]
    parts = [total[:, e - n : e] for e, n in zip(ends, sizes)]
    project_all, wexp_all, kernel_all = parts[0], parts[1].T, parts[2]
    grad_wsq_all, grad_wexc_all, gain_all = parts[3], parts[4].T, parts[5][:chans, 0]
    return (
        output,
        grad_in.astype(jnp.bfloat16),
        gain_all,
        wexp_all,
        kernel_all,
        grad_wsq_all,
        grad_wexc_all,
        project_all,
    )


def solution(mesh):
    placed = (
        P("dp", None, "row", "col"),
        P(),
        P(),
        P(),
        P(),
        P(),
        P(),
        P("dp", None, "row", "col"),
    )
    return jax.shard_map(
        local,
        mesh=mesh,
        in_specs=placed,
        out_specs=(
            P("dp", None, "row", "col"),
            P("dp", None, "row", "col"),
            P(),
            P(),
            P(),
            P(),
            P(),
            P(),
        ),
        check_vma=False,
    )
```

```python
import jax
import jax.numpy as jnp
from jax import lax
from jax.experimental import pallas as pl
from jax.experimental.pallas import tpu as pltpu
from jax.sharding import PartitionSpec as P

EPS = 1e-06
HIGH = lax.Precision.HIGHEST

MESH = pl.DeviceIdType.MESH

def sum_kernel(v_ref, out_ref, mate_buf, acc1, group_buf, acc2, deep_buf, send, recv):
    groups, deep = v_ref.shape[1], v_ref.shape[2]
    half_cols = lax.axis_size("col") // 2
    d, w, c = (lax.axis_index(a) for a in ("dp", "row", "col"))
    core = lax.rem(c, 2)
    g = w * half_cols + c // 2

    def mate():
        return (d, w, c + 1 - 2 * core)

    def peer(s):
        at = lax.rem(g + s, groups)
        return at, (d, at // half_cols, lax.rem(at, half_cols) * 2 + core)

    def layer(s):
        at = lax.rem(d + s, deep)
        return at, (at, w, c)

    barrier = pltpu.get_barrier_semaphore()
    others = [mate()] + [peer(s)[1] for s in range(1, groups)]
    others += [layer(s)[1] for s in range(1, deep)]
    for other in others:
        pl.semaphore_signal(barrier, inc=1, device_id=other, device_id_type=MESH)
    pl.semaphore_wait(barrier, len(others))

    def copy(src, dst, n, to):
        return pltpu.make_async_remote_copy(
            src_ref=src,
            dst_ref=dst,
            send_sem=send.at[n],
            recv_sem=recv.at[n],
            device_id=to,
            device_id_type=MESH,
        )

    def run(copies):
        for one in copies:
            one.start()
        for one in copies:
            one.wait()

    run([copy(v_ref.at[1 - core], mate_buf, 0, mate())])
    acc1[...] = v_ref[core] + mate_buf[...]
    n = 0
    moves = []
    for s in range(1, groups):
        at, to = peer(s)
        moves.append(copy(acc1.at[at], group_buf.at[s - 1], n + s, to))
    run(moves)
    part = acc1[g]
    for s in range(1, groups):
        part = part + group_buf[s - 1]
    acc2[...] = part
    n += groups - 1
    moves = []
    for s in range(1, deep):
        at, to = layer(s)
        moves.append(copy(acc2.at[at], deep_buf.at[s - 1], n + s, to))
    run(moves)
    part = acc2[d]
    for s in range(1, deep):
        part = part + deep_buf[s - 1]
    out_ref[core, g, d] = part
    n += deep - 1
    mine = out_ref.at[core, g, d]
    run([copy(mine, mine, n + s, layer(s)[1]) for s in range(1, deep)])
    n += deep - 1
    mine = out_ref.at[core, g]
    run([copy(mine, mine, n + s, peer(s)[1]) for s in range(1, groups)])
    n += groups
    mine = out_ref.at[core]
    run([copy(mine, mine, n, mate())])


def sum_all(values):
    rows, cols = values.shape
    groups = lax.axis_size("row") * (lax.axis_size("col") // 2)
    deep = lax.axis_size("dp")
    each = -(-rows // (2 * groups * deep))
    wide = -(-cols // 128) * 128
    full = 2 * groups * deep * each
    laid = jnp.pad(values, ((0, full - rows), (0, wide - cols)))
    laid = laid.reshape(2, groups, deep, each, wide)
    f32 = jnp.float32
    count = 2 * (1 + groups - 1 + deep - 1) + 1
    total = pl.pallas_call(
        sum_kernel,
        out_shape=jax.ShapeDtypeStruct(laid.shape, f32),
        in_specs=[pl.BlockSpec(memory_space=pltpu.VMEM)],
        out_specs=pl.BlockSpec(memory_space=pltpu.VMEM),
        scratch_shapes=[
            pltpu.VMEM((groups, deep, each, wide), f32),
            pltpu.VMEM((groups, deep, each, wide), f32),
            pltpu.VMEM((max(groups - 1, 1), deep, each, wide), f32),
            pltpu.VMEM((deep, each, wide), f32),
            pltpu.VMEM((max(deep - 1, 1), each, wide), f32),
            pltpu.SemaphoreType.DMA((count,)),
            pltpu.SemaphoreType.DMA((count,)),
        ],
        compiler_params=pltpu.CompilerParams(
            collective_id=0, has_side_effects=True, vmem_limit_bytes=48 << 20
        ),
        name="sum_grads",
    )(laid)
    return total.reshape(full, wide)[:rows, :cols]


def greet(others):
    barrier = pltpu.get_barrier_semaphore()
    for other in others:
        pl.semaphore_signal(barrier, inc=1, device_id=other, device_id_type=MESH)
    pl.semaphore_wait(barrier, len(others))


def halo_kernel(rows_ref, cols_ref, got_rows, got_cols, send, recv):
    d, w, c = (lax.axis_index(a) for a in ("dp", "row", "col"))
    count, wide = lax.axis_size("row"), lax.axis_size("col")

    def at(drow, dcol):
        return (d, lax.rem(w + drow + count, count), lax.rem(c + dcol + wide, wide))

    plan = [
        (rows_ref.at[1], got_rows.at[0], at(1, 0)),
        (rows_ref.at[0], got_rows.at[1], at(-1, 0)),
    ]
    for side, dcol in enumerate((1, -1)):
        for drow in (-1, 0, 1):
            slot = got_cols.at[side * 3 + 1 - drow]
            plan.append((cols_ref.at[1 - side], slot, at(drow, dcol)))
    greet([to for _, _, to in plan])
    copies = [
        pltpu.make_async_remote_copy(
            src_ref=src,
            dst_ref=dst,
            send_sem=send.at[n],
            recv_sem=recv.at[n],
            device_id=to,
            device_id_type=MESH,
        )
        for n, (src, dst, to) in enumerate(plan)
    ]
    for copy in copies:
        copy.start()
    for copy in copies:
        copy.wait()


def with_halo(shard, number):
    _, chans, rows, cols = shard.shape
    count, wide = lax.axis_size("row"), lax.axis_size("col")
    w, c = lax.axis_index("row"), lax.axis_index("col")
    own = shard[0]
    tall = -(-rows // 16) * 16
    edge_rows = jnp.stack([own[:, 0, :], own[:, rows - 1, :]])
    edge_cols = jnp.stack([own[:, :, 0].T, own[:, :, cols - 1].T])
    edge_cols = jnp.pad(edge_cols, ((0, 0), (0, tall - rows), (0, 0)))
    got_rows, got_cols = pl.pallas_call(
        halo_kernel,
        out_shape=[
            jax.ShapeDtypeStruct(edge_rows.shape, shard.dtype),
            jax.ShapeDtypeStruct((6, tall, chans), shard.dtype),
        ],
        in_specs=[pl.BlockSpec(memory_space=pltpu.VMEM)] * 2,
        out_specs=[pl.BlockSpec(memory_space=pltpu.VMEM)] * 2,
        scratch_shapes=[pltpu.SemaphoreType.DMA((8,)), pltpu.SemaphoreType.DMA((8,))],
        compiler_params=pltpu.CompilerParams(
            collective_id=number, has_side_effects=True, vmem_limit_bytes=48 << 20
        ),
        name="halo",
    )(edge_rows, edge_cols)
    up, down = w > 0, w < count - 1
    zero = jnp.zeros((), shard.dtype)
    above = jnp.where(up, got_rows[0], zero)[:, None, :]
    below = jnp.where(down, got_rows[1], zero)[:, None, :]

    def side(got, there):
        top = jnp.where(up, got[0, rows - 1 : rows], zero)
        bottom = jnp.where(down, got[2, 0:1], zero)
        whole = jnp.concatenate([top, got[1, :rows], bottom], axis=0)
        return jnp.where(there, whole, zero).T[:, :, None]

    mid = jnp.concatenate([above, own, below], axis=1)
    left, right = side(got_cols[:3], c > 0), side(got_cols[3:], c < wide - 1)
    return jnp.concatenate([left, mid, right], axis=2)[None]


def sample_kernel(v_ref, out_ref, buf, send, recv):
    d, w, c = (lax.axis_index(a) for a in ("dp", "row", "col"))
    wide = lax.axis_size("col")
    group = lax.axis_size("row") * wide
    me = w * wide + c
    others = []
    for s in range(1, group):
        at = lax.rem(me + s, group)
        others.append((d, at // wide, lax.rem(at, wide)))
    greet(others)
    copies = [
        pltpu.make_async_remote_copy(
            src_ref=v_ref,
            dst_ref=buf.at[me],
            send_sem=send.at[n],
            recv_sem=recv.at[n],
            device_id=to,
            device_id_type=MESH,
        )
        for n, to in enumerate(others)
    ]
    for copy in copies:
        copy.start()
    buf[me] = v_ref[...]
    for copy in copies:
        copy.wait()
    total = buf[0]
    for s in range(1, group):
        total = total + buf[s]
    out_ref[...] = total


def sample_sum(values):
    group = lax.axis_size("row") * lax.axis_size("col")
    return pl.pallas_call(
        sample_kernel,
        out_shape=jax.ShapeDtypeStruct(values.shape, values.dtype),
        in_specs=[pl.BlockSpec(memory_space=pltpu.VMEM)],
        out_specs=pl.BlockSpec(memory_space=pltpu.VMEM),
        scratch_shapes=[
            pltpu.VMEM((group, *values.shape), values.dtype),
            pltpu.SemaphoreType.DMA((group - 1,)),
            pltpu.SemaphoreType.DMA((group - 1,)),
        ],
        compiler_params=pltpu.CompilerParams(
            collective_id=3, has_side_effects=True, vmem_limit_bytes=48 << 20
        ),
        name="sample_sum",
    )(values)


def silu_slope(value):
    sig = jax.nn.sigmoid(value)
    return sig * (1.0 + value * (1.0 - sig))


def normalize(inputs, norm_gain):
    widened = inputs.astype(jnp.float32)
    inverse = lax.rsqrt(jnp.mean(widened * widened, axis=1, keepdims=True) + EPS)
    normed = widened * inverse
    scaled = (normed * norm_gain[None, :, None, None]).astype(jnp.bfloat16)
    return (normed, inverse, scaled)


def expand(scaled, w_expand):
    return jnp.einsum("bchw,ce->behw", scaled, w_expand, preferred_element_type=jnp.float32)


def depthwise(hidden_pad, kernel, out_rows, out_cols):
    total = jnp.zeros((hidden_pad.shape[0], hidden_pad.shape[1], out_rows, out_cols), jnp.float32)
    for tap in range(9):
        drow, dcol = (tap // 3, tap % 3)
        total = (
            total
            + kernel[:, tap][None, :, None, None]
            * hidden_pad[:, :, drow : drow + out_rows, dcol : dcol + out_cols]
        )
    return total


def local(inputs, norm_gain, w_expand, kernel, w_squeeze, w_excite, w_project, cotangent):
    batch, chans, rows, cols = inputs.shape
    pixels = rows * cols * lax.axis_size("row") * lax.axis_size("col")
    normed, inverse, scaled = normalize(inputs, norm_gain)
    pre = expand(scaled, w_expand)
    hidden = jax.nn.silu(pre).astype(jnp.bfloat16)
    hidden_pad = with_halo(hidden, 1)
    conv = depthwise(hidden_pad, kernel, rows, cols)
    act = jax.nn.silu(conv)
    grad_gated = jnp.einsum(
        "bchw,ec->behw", cotangent, w_project, preferred_element_type=jnp.float32
    )
    sums = sample_sum(
        jnp.concatenate([jnp.sum(act, axis=(2, 3)), jnp.sum(grad_gated * act, axis=(2, 3))])
    )
    pooled = sums[:batch] / pixels
    squeeze_pre = jnp.dot(pooled, w_squeeze, precision=HIGH)
    squeezed = jax.nn.silu(squeeze_pre)
    excite_pre = jnp.dot(squeezed, w_excite, precision=HIGH)
    excite = jax.nn.sigmoid(excite_pre)
    gated = (act * excite[:, :, None, None]).astype(jnp.bfloat16)
    proj = jnp.einsum("behw,ec->bchw", gated, w_project, preferred_element_type=jnp.float32)
    output = (inputs.astype(jnp.float32) + proj).astype(jnp.bfloat16)
    grad_project = jnp.einsum("behw,bchw->ec", gated, cotangent, preferred_element_type=jnp.float32)
    grad_excite = sums[batch:]
    grad_epre = grad_excite * excite * (1.0 - excite)
    grad_wexc = jnp.einsum("bs,be->se", squeezed, grad_epre, precision=HIGH)
    grad_spre = jnp.einsum("be,se->bs", grad_epre, w_excite, precision=HIGH) * silu_slope(
        squeeze_pre
    )
    grad_wsq = jnp.einsum("be,bs->es", pooled, grad_spre, precision=HIGH)
    grad_pooled = jnp.einsum("bs,es->be", grad_spre, w_squeeze, precision=HIGH)
    grad_act = grad_gated * excite[:, :, None, None] + (grad_pooled / pixels)[:, :, None, None]
    grad_conv = (grad_act * silu_slope(conv)).astype(jnp.bfloat16)
    grad_pad = with_halo(grad_conv, 2)
    grad_hidden = jnp.zeros(pre.shape, jnp.float32)
    taps = []
    for tap in range(9):
        drow, dcol = (tap // 3, tap % 3)
        grad_hidden = (
            grad_hidden
            + kernel[:, tap][None, :, None, None]
            * grad_pad[:, :, 2 - drow : 2 - drow + rows, 2 - dcol : 2 - dcol + cols]
        )
        taps.append(
            jnp.sum(
                grad_conv.astype(jnp.float32)
                * hidden_pad[:, :, drow : drow + rows, dcol : dcol + cols].astype(jnp.float32),
                axis=(0, 2, 3),
            )
        )
    grad_kernel = jnp.stack(taps, axis=1)
    grad_pre = (grad_hidden * silu_slope(pre)).astype(jnp.bfloat16)
    grad_wexp = jnp.einsum("bchw,behw->ce", scaled, grad_pre, preferred_element_type=jnp.float32)
    grad_scaled = jnp.einsum(
        "ce,behw->bchw", w_expand, grad_pre, preferred_element_type=jnp.float32
    )
    grad_gain = jnp.sum(grad_scaled * normed, axis=(0, 2, 3))
    grad_normed = grad_scaled * norm_gain[None, :, None, None]
    grad_in = inverse * (
        grad_normed - normed * jnp.mean(grad_normed * normed, axis=1, keepdims=True)
    ) + cotangent.astype(jnp.float32)
    lead = jnp.logical_and(lax.axis_index("row") == 0, lax.axis_index("col") == 0)
    keep = lead.astype(jnp.float32)
    hidden_n = grad_project.shape[0]
    pieces = [
        grad_project,
        grad_wexp.T,
        grad_kernel,
        grad_wsq * keep,
        grad_wexc.T * keep,
        jnp.pad(grad_gain, (0, hidden_n - chans))[:, None],
    ]
    sizes = [p.shape[1] for p in pieces]
    total = sum_all(jnp.concatenate(pieces, axis=1))
    ends = [sum(sizes[: n + 1]) for n in range(len(sizes))]
    parts = [total[:, e - n : e] for e, n in zip(ends, sizes)]
    project_all, wexp_all, kernel_all = parts[0], parts[1].T, parts[2]
    grad_wsq_all, grad_wexc_all, gain_all = parts[3], parts[4].T, parts[5][:chans, 0]
    return (
        output,
        grad_in.astype(jnp.bfloat16),
        gain_all,
        wexp_all,
        kernel_all,
        grad_wsq_all,
        grad_wexc_all,
        project_all,
    )


def solution(mesh):
    placed = (
        P("dp", None, "row", "col"),
        P(),
        P(),
        P(),
        P(),
        P(),
        P(),
        P("dp", None, "row", "col"),
    )
    return jax.shard_map(
        local,
        mesh=mesh,
        in_specs=placed,
        out_specs=(
            P("dp", None, "row", "col"),
            P("dp", None, "row", "col"),
            P(),
            P(),
            P(),
            P(),
            P(),
            P(),
        ),
        check_vma=False,
    )
```

```python
import jax
import jax.numpy as jnp
from jax import lax
from jax.experimental import pallas as pl
from jax.experimental.pallas import tpu as pltpu
from jax.sharding import PartitionSpec as P

EPS = 1e-06
HIGH = lax.Precision.HIGHEST

MESH = pl.DeviceIdType.MESH

def sum_kernel(v_ref, out_ref, mate_buf, acc1, group_buf, acc2, deep_buf, send, recv):
    groups, deep = v_ref.shape[1], v_ref.shape[2]
    half_cols = lax.axis_size("col") // 2
    d, w, c = (lax.axis_index(a) for a in ("dp", "row", "col"))
    core = lax.rem(c, 2)
    g = w * half_cols + c // 2

    def mate():
        return (d, w, c + 1 - 2 * core)

    def peer(s):
        at = lax.rem(g + s, groups)
        return at, (d, at // half_cols, lax.rem(at, half_cols) * 2 + core)

    def layer(s):
        at = lax.rem(d + s, deep)
        return at, (at, w, c)

    barrier = pltpu.get_barrier_semaphore()
    others = [mate()] + [peer(s)[1] for s in range(1, groups)]
    others += [layer(s)[1] for s in range(1, deep)]
    for other in others:
        pl.semaphore_signal(barrier, inc=1, device_id=other, device_id_type=MESH)
    pl.semaphore_wait(barrier, len(others))

    width = chunk_of(v_ref.shape[-1])
    chunks = range(v_ref.shape[-1] // width)
    sent = []

    def go(src, dst, n, k, to):
        copy = pltpu.make_async_remote_copy(
            src_ref=src,
            dst_ref=dst,
            send_sem=send.at[n, k],
            recv_sem=recv.at[n, k],
            device_id=to,
            device_id_type=MESH,
        )
        copy.start()
        sent.append(copy)
        return copy

    cuts = [pl.ds(k * width, width) for k in chunks]
    arriving = []
    for k in chunks:
        src = v_ref.at[1 - core, :, :, :, cuts[k]]
        arriving.append([go(src, mate_buf.at[:, :, :, cuts[k]], 0, k, mate())])

    def landed(k):
        for copy in arriving[k]:
            copy.wait_recv()
        arriving[k] = []

    for k in chunks:
        landed(k)
        cut = cuts[k]
        acc1[:, :, :, cut] = v_ref[core, :, :, :, cut] + mate_buf[:, :, :, cut]
        for s in range(1, groups):
            at, to = peer(s)
            src, dst = acc1.at[at, :, :, cut], group_buf.at[s - 1, :, :, cut]
            arriving[k].append(go(src, dst, s, k, to))
    n = groups - 1
    for k in chunks:
        landed(k)
        cut = cuts[k]
        part = acc1[g, :, :, cut]
        for s in range(1, groups):
            part = part + group_buf[s - 1, :, :, cut]
        acc2[:, :, cut] = part
        for s in range(1, deep):
            at, to = layer(s)
            src, dst = acc2.at[at, :, cut], deep_buf.at[s - 1, :, cut]
            arriving[k].append(go(src, dst, n + s, k, to))
    n += deep - 1
    for k in chunks:
        landed(k)
        cut = cuts[k]
        part = acc2[d, :, cut]
        for s in range(1, deep):
            part = part + deep_buf[s - 1, :, cut]
        out_ref[core, g, d, :, cut] = part
        mine = out_ref.at[core, g, d, :, cut]
        for s in range(1, deep):
            arriving[k].append(go(mine, mine, n + s, k, layer(s)[1]))
    n += deep - 1
    for k in chunks:
        landed(k)
        mine = out_ref.at[core, g, :, :, cuts[k]]
        for s in range(1, groups):
            arriving[k].append(go(mine, mine, n + s, k, peer(s)[1]))
    n += groups
    for k in chunks:
        landed(k)
        mine = out_ref.at[core, :, :, :, cuts[k]]
        arriving[k].append(go(mine, mine, n, k, mate()))
    for k in chunks:
        landed(k)
    for copy in sent:
        copy.wait_send()


def chunk_of(wide):
    return 256 if wide % 256 == 0 else wide


def sum_all(values):
    rows, cols = values.shape
    groups = lax.axis_size("row") * (lax.axis_size("col") // 2)
    deep = lax.axis_size("dp")
    each = -(-rows // (2 * groups * deep))
    wide = -(-cols // 128) * 128
    full = 2 * groups * deep * each
    laid = jnp.pad(values, ((0, full - rows), (0, wide - cols)))
    laid = laid.reshape(2, groups, deep, each, wide)
    f32 = jnp.float32
    count = 2 * (1 + groups - 1 + deep - 1) + 1
    total = pl.pallas_call(
        sum_kernel,
        out_shape=jax.ShapeDtypeStruct(laid.shape, f32),
        in_specs=[pl.BlockSpec(memory_space=pltpu.VMEM)],
        out_specs=pl.BlockSpec(memory_space=pltpu.VMEM),
        scratch_shapes=[
            pltpu.VMEM((groups, deep, each, wide), f32),
            pltpu.VMEM((groups, deep, each, wide), f32),
            pltpu.VMEM((max(groups - 1, 1), deep, each, wide), f32),
            pltpu.VMEM((deep, each, wide), f32),
            pltpu.VMEM((max(deep - 1, 1), each, wide), f32),
            pltpu.SemaphoreType.DMA((count, wide // chunk_of(wide))),
            pltpu.SemaphoreType.DMA((count, wide // chunk_of(wide))),
        ],
        compiler_params=pltpu.CompilerParams(
            collective_id=0, has_side_effects=True, vmem_limit_bytes=48 << 20
        ),
        name="sum_grads",
    )(laid)
    return total.reshape(full, wide)[:rows, :cols]


def greet(others):
    barrier = pltpu.get_barrier_semaphore()
    for other in others:
        pl.semaphore_signal(barrier, inc=1, device_id=other, device_id_type=MESH)
    pl.semaphore_wait(barrier, len(others))


def halo_kernel(rows_ref, cols_ref, got_rows, got_cols, send, recv):
    d, w, c = (lax.axis_index(a) for a in ("dp", "row", "col"))
    count, wide = lax.axis_size("row"), lax.axis_size("col")

    def at(drow, dcol):
        return (d, lax.rem(w + drow + count, count), lax.rem(c + dcol + wide, wide))

    up, down, left, right = w > 0, w < count - 1, c > 0, c < wide - 1
    rows_there = {-1: up, 0: True, 1: down}
    cols_there = {-1: left, 0: True, 1: right}
    plan = [
        (rows_ref.at[1], got_rows.at[0], 1, 0),
        (rows_ref.at[0], got_rows.at[1], -1, 0),
    ]
    for side, dcol in enumerate((1, -1)):
        for drow in (-1, 0, 1):
            slot = got_cols.at[side * 3 + 1 - drow]
            plan.append((cols_ref.at[1 - side], slot, drow, dcol))
    greet([at(drow, dcol) for _, _, drow, dcol in plan])

    def there(drow, dcol):
        return jnp.logical_and(rows_there[drow], cols_there[dcol])

    copies = [
        pltpu.make_async_remote_copy(
            src_ref=src,
            dst_ref=dst,
            send_sem=send.at[n],
            recv_sem=recv.at[n],
            device_id=at(drow, dcol),
            device_id_type=MESH,
        )
        for n, (src, dst, drow, dcol) in enumerate(plan)
    ]
    for copy, (_, _, drow, dcol) in zip(copies, plan):
        pl.when(there(drow, dcol))(copy.start)
    for copy, (_, _, drow, dcol) in zip(copies, plan):
        pl.when(there(-drow, -dcol))(copy.wait_recv)
    for copy, (_, _, drow, dcol) in zip(copies, plan):
        pl.when(there(drow, dcol))(copy.wait_send)


def with_halo(shard, number):
    _, chans, rows, cols = shard.shape
    count, wide = lax.axis_size("row"), lax.axis_size("col")
    w, c = lax.axis_index("row"), lax.axis_index("col")
    own = shard[0].transpose(1, 2, 0)
    tall = -(-rows // 16) * 16
    edge_rows = jnp.stack([own[0], own[rows - 1]])
    edge_cols = jnp.stack([own[:, 0], own[:, cols - 1]])
    edge_cols = jnp.pad(edge_cols, ((0, 0), (0, tall - rows), (0, 0)))
    got_rows, got_cols = pl.pallas_call(
        halo_kernel,
        out_shape=[
            jax.ShapeDtypeStruct(edge_rows.shape, shard.dtype),
            jax.ShapeDtypeStruct((6, tall, chans), shard.dtype),
        ],
        in_specs=[pl.BlockSpec(memory_space=pltpu.VMEM)] * 2,
        out_specs=[pl.BlockSpec(memory_space=pltpu.VMEM)] * 2,
        scratch_shapes=[pltpu.SemaphoreType.DMA((8,)), pltpu.SemaphoreType.DMA((8,))],
        compiler_params=pltpu.CompilerParams(
            collective_id=number, has_side_effects=True, vmem_limit_bytes=48 << 20
        ),
        name="halo",
    )(edge_rows, edge_cols)
    up, down = w > 0, w < count - 1
    zero = jnp.zeros((), shard.dtype)
    above = jnp.where(up, got_rows[0], zero)[None]
    below = jnp.where(down, got_rows[1], zero)[None]

    def side(got, there):
        top = jnp.where(up, got[0, rows - 1 : rows], zero)
        bottom = jnp.where(down, got[2, 0:1], zero)
        whole = jnp.concatenate([top, got[1, :rows], bottom], axis=0)
        return jnp.where(there, whole, zero)[:, None]

    mid = jnp.concatenate([above, own, below], axis=0)
    left, right = side(got_cols[:3], c > 0), side(got_cols[3:], c < wide - 1)
    return jnp.concatenate([left, mid, right], axis=1).transpose(2, 0, 1)[None]


def sample_kernel(v_ref, out_ref, buf, send, recv):
    d, w, c = (lax.axis_index(a) for a in ("dp", "row", "col"))
    wide = lax.axis_size("col")
    group = lax.axis_size("row") * wide
    me = w * wide + c
    others = []
    for s in range(1, group):
        at = lax.rem(me + s, group)
        others.append((d, at // wide, lax.rem(at, wide)))
    greet(others)
    copies = [
        pltpu.make_async_remote_copy(
            src_ref=v_ref,
            dst_ref=buf.at[me],
            send_sem=send.at[n],
            recv_sem=recv.at[n],
            device_id=to,
            device_id_type=MESH,
        )
        for n, to in enumerate(others)
    ]
    for copy in copies:
        copy.start()
    buf[me] = v_ref[...]
    for copy in copies:
        copy.wait()
    total = buf[0]
    for s in range(1, group):
        total = total + buf[s]
    out_ref[...] = total


def sample_sum(values):
    group = lax.axis_size("row") * lax.axis_size("col")
    return pl.pallas_call(
        sample_kernel,
        out_shape=jax.ShapeDtypeStruct(values.shape, values.dtype),
        in_specs=[pl.BlockSpec(memory_space=pltpu.VMEM)],
        out_specs=pl.BlockSpec(memory_space=pltpu.VMEM),
        scratch_shapes=[
            pltpu.VMEM((group, *values.shape), values.dtype),
            pltpu.SemaphoreType.DMA((group - 1,)),
            pltpu.SemaphoreType.DMA((group - 1,)),
        ],
        compiler_params=pltpu.CompilerParams(
            collective_id=3, has_side_effects=True, vmem_limit_bytes=48 << 20
        ),
        name="sample_sum",
    )(values)


def silu_slope(value):
    sig = jax.nn.sigmoid(value)
    return sig * (1.0 + value * (1.0 - sig))


def normalize(inputs, norm_gain):
    widened = inputs.astype(jnp.float32)
    inverse = lax.rsqrt(jnp.mean(widened * widened, axis=1, keepdims=True) + EPS)
    normed = widened * inverse
    scaled = (normed * norm_gain[None, :, None, None]).astype(jnp.bfloat16)
    return (normed, inverse, scaled)


def expand(scaled, w_expand):
    return jnp.einsum("bchw,ce->behw", scaled, w_expand, preferred_element_type=jnp.float32)


def depthwise(hidden_pad, kernel, out_rows, out_cols):
    total = jnp.zeros((hidden_pad.shape[0], hidden_pad.shape[1], out_rows, out_cols), jnp.float32)
    for tap in range(9):
        drow, dcol = (tap // 3, tap % 3)
        total = (
            total
            + kernel[:, tap][None, :, None, None]
            * hidden_pad[:, :, drow : drow + out_rows, dcol : dcol + out_cols]
        )
    return total


def local(inputs, norm_gain, w_expand, kernel, w_squeeze, w_excite, w_project, cotangent):
    batch, chans, rows, cols = inputs.shape
    pixels = rows * cols * lax.axis_size("row") * lax.axis_size("col")
    normed, inverse, scaled = normalize(inputs, norm_gain)
    pre = expand(scaled, w_expand)
    hidden = jax.nn.silu(pre).astype(jnp.bfloat16)
    hidden_pad = with_halo(hidden, 1)
    conv = depthwise(hidden_pad, kernel, rows, cols)
    act = jax.nn.silu(conv)
    grad_gated = jnp.einsum(
        "bchw,ec->behw", cotangent, w_project, preferred_element_type=jnp.float32
    )
    sums = sample_sum(
        jnp.concatenate([jnp.sum(act, axis=(2, 3)), jnp.sum(grad_gated * act, axis=(2, 3))])
    )
    pooled = sums[:batch] / pixels
    squeeze_pre = jnp.dot(pooled, w_squeeze, precision=HIGH)
    squeezed = jax.nn.silu(squeeze_pre)
    excite_pre = jnp.dot(squeezed, w_excite, precision=HIGH)
    excite = jax.nn.sigmoid(excite_pre)
    gated = (act * excite[:, :, None, None]).astype(jnp.bfloat16)
    proj = jnp.einsum("behw,ec->bchw", gated, w_project, preferred_element_type=jnp.float32)
    output = (inputs.astype(jnp.float32) + proj).astype(jnp.bfloat16)
    grad_project = jnp.einsum("bchw,behw->ce", cotangent, gated, preferred_element_type=jnp.float32)
    grad_excite = sums[batch:]
    grad_epre = grad_excite * excite * (1.0 - excite)
    grad_wexc = jnp.einsum("bs,be->se", squeezed, grad_epre, precision=HIGH)
    grad_spre = jnp.einsum("be,se->bs", grad_epre, w_excite, precision=HIGH) * silu_slope(
        squeeze_pre
    )
    grad_wsq = jnp.einsum("bs,be->se", grad_spre, pooled, precision=HIGH)
    grad_pooled = jnp.einsum("bs,es->be", grad_spre, w_squeeze, precision=HIGH)
    grad_act = grad_gated * excite[:, :, None, None] + (grad_pooled / pixels)[:, :, None, None]
    grad_conv = (grad_act * silu_slope(conv)).astype(jnp.bfloat16)
    grad_pad = with_halo(grad_conv, 2)
    grad_hidden = jnp.zeros(pre.shape, jnp.float32)
    taps = []
    for tap in range(9):
        drow, dcol = (tap // 3, tap % 3)
        grad_hidden = (
            grad_hidden
            + kernel[:, tap][None, :, None, None]
            * grad_pad[:, :, 2 - drow : 2 - drow + rows, 2 - dcol : 2 - dcol + cols]
        )
        taps.append(
            jnp.sum(
                grad_conv.astype(jnp.float32)
                * hidden_pad[:, :, drow : drow + rows, dcol : dcol + cols].astype(jnp.float32),
                axis=(0, 2, 3),
            )
        )
    grad_kernel = jnp.stack(taps, axis=0)
    grad_pre = (grad_hidden * silu_slope(pre)).astype(jnp.bfloat16)
    grad_wexp = jnp.einsum("bchw,behw->ce", scaled, grad_pre, preferred_element_type=jnp.float32)
    grad_scaled = jnp.einsum(
        "ce,behw->bchw", w_expand, grad_pre, preferred_element_type=jnp.float32
    )
    grad_gain = jnp.sum(grad_scaled * normed, axis=(0, 2, 3))
    grad_normed = grad_scaled * norm_gain[None, :, None, None]
    grad_in = inverse * (
        grad_normed - normed * jnp.mean(grad_normed * normed, axis=1, keepdims=True)
    ) + cotangent.astype(jnp.float32)
    lead = jnp.logical_and(lax.axis_index("row") == 0, lax.axis_index("col") == 0)
    keep = lead.astype(jnp.float32)
    hidden_n = grad_project.shape[1]
    pieces = [
        grad_project,
        grad_wexp,
        grad_kernel,
        grad_wsq * keep,
        grad_wexc * keep,
        jnp.pad(grad_gain, (0, hidden_n - chans))[None],
    ]
    sizes = [p.shape[0] for p in pieces]
    total = sum_all(jnp.concatenate(pieces, axis=0))
    ends = [sum(sizes[: n + 1]) for n in range(len(sizes))]
    parts = [total[e - n : e] for e, n in zip(ends, sizes)]
    project_all, wexp_all, kernel_all = parts[0].T, parts[1], parts[2].T
    grad_wsq_all, grad_wexc_all, gain_all = parts[3].T, parts[4], parts[5][0, :chans]
    return (
        output,
        grad_in.astype(jnp.bfloat16),
        gain_all,
        wexp_all,
        kernel_all,
        grad_wsq_all,
        grad_wexc_all,
        project_all,
    )


def solution(mesh):
    placed = (
        P("dp", None, "row", "col"),
        P(),
        P(),
        P(),
        P(),
        P(),
        P(),
        P("dp", None, "row", "col"),
    )
    return jax.shard_map(
        local,
        mesh=mesh,
        in_specs=placed,
        out_specs=(
            P("dp", None, "row", "col"),
            P("dp", None, "row", "col"),
            P(),
            P(),
            P(),
            P(),
            P(),
            P(),
        ),
        check_vma=False,
    )
```

```python
import jax
import jax.numpy as jnp
from jax import lax
from jax.experimental import pallas as pl
from jax.experimental.pallas import tpu as pltpu
from jax.sharding import PartitionSpec as P

EPS = 1e-06
HIGH = lax.Precision.HIGHEST

MESH = pl.DeviceIdType.MESH

def sum_kernel(v_ref, out_ref, mate_buf, acc1, group_buf, acc2, deep_buf, send, recv):
    groups, deep = v_ref.shape[1], v_ref.shape[2]
    half_cols = lax.axis_size("col") // 2
    d, w, c = (lax.axis_index(a) for a in ("dp", "row", "col"))
    core = lax.rem(c, 2)
    g = w * half_cols + c // 2

    def mate():
        return (d, w, c + 1 - 2 * core)

    def peer(s):
        at = lax.rem(g + s, groups)
        return at, (d, at // half_cols, lax.rem(at, half_cols) * 2 + core)

    def layer(s):
        at = lax.rem(d + s, deep)
        return at, (at, w, c)

    barrier = pltpu.get_barrier_semaphore()
    others = [mate()] + [peer(s)[1] for s in range(1, groups)]
    others += [layer(s)[1] for s in range(1, deep)]
    for other in others:
        pl.semaphore_signal(barrier, inc=1, device_id=other, device_id_type=MESH)
    pl.semaphore_wait(barrier, len(others))

    each = v_ref.shape[3]
    step = 8 * -(-each // 24)
    starts = range(0, each, step)
    chunks = range(len(starts))
    sent = []

    def go(src, dst, n, k, to):
        copy = pltpu.make_async_remote_copy(
            src_ref=src,
            dst_ref=dst,
            send_sem=send.at[n, k],
            recv_sem=recv.at[n, k],
            device_id=to,
            device_id_type=MESH,
        )
        copy.start()
        sent.append(copy)
        return copy

    cuts = [pl.ds(at, min(step, each - at)) for at in starts]
    arriving = []
    for k in chunks:
        src = v_ref.at[1 - core, :, :, cuts[k]]
        arriving.append([go(src, mate_buf.at[:, :, cuts[k]], 0, k, mate())])

    def landed(k):
        for copy in arriving[k]:
            copy.wait_recv()
        arriving[k] = []

    for k in chunks:
        landed(k)
        cut = cuts[k]
        acc1[:, :, cut] = v_ref[core, :, :, cut] + mate_buf[:, :, cut]
        for s in range(1, groups):
            at, to = peer(s)
            src, dst = acc1.at[at, :, cut], group_buf.at[s - 1, :, cut]
            arriving[k].append(go(src, dst, s, k, to))
    n = groups - 1
    for k in chunks:
        landed(k)
        cut = cuts[k]
        part = acc1[g, :, cut]
        for s in range(1, groups):
            part = part + group_buf[s - 1, :, cut]
        acc2[:, cut] = part
        for s in range(1, deep):
            at, to = layer(s)
            src, dst = acc2.at[at, cut], deep_buf.at[s - 1, cut]
            arriving[k].append(go(src, dst, n + s, k, to))
    n += deep - 1
    for k in chunks:
        landed(k)
        cut = cuts[k]
        part = acc2[d, cut]
        for s in range(1, deep):
            part = part + deep_buf[s - 1, cut]
        out_ref[core, g, d, cut] = part
        mine = out_ref.at[core, g, d, cut]
        for s in range(1, deep):
            arriving[k].append(go(mine, mine, n + s, k, layer(s)[1]))
    n += deep - 1
    for k in chunks:
        landed(k)
        mine = out_ref.at[core, g, :, cuts[k]]
        for s in range(1, groups):
            arriving[k].append(go(mine, mine, n + s, k, peer(s)[1]))
    n += groups
    for k in chunks:
        landed(k)
        mine = out_ref.at[core, :, :, cuts[k]]
        arriving[k].append(go(mine, mine, n, k, mate()))
    for k in chunks:
        landed(k)
    for copy in sent:
        copy.wait_send()


def chunk_of(wide):
    return 256 if wide % 256 == 0 else wide


def sum_all(values):
    rows, cols = values.shape
    groups = lax.axis_size("row") * (lax.axis_size("col") // 2)
    deep = lax.axis_size("dp")
    each = 8 * -(-rows // (16 * groups * deep))
    wide = -(-cols // 128) * 128
    chunks = -(-each // (8 * -(-each // 24)))
    full = 2 * groups * deep * each
    laid = jnp.pad(values, ((0, full - rows), (0, wide - cols)))
    laid = laid.reshape(2, groups, deep, each, wide)
    f32 = jnp.float32
    count = 2 * (1 + groups - 1 + deep - 1) + 1
    total = pl.pallas_call(
        sum_kernel,
        out_shape=jax.ShapeDtypeStruct(laid.shape, f32),
        in_specs=[pl.BlockSpec(memory_space=pltpu.VMEM)],
        out_specs=pl.BlockSpec(memory_space=pltpu.VMEM),
        scratch_shapes=[
            pltpu.VMEM((groups, deep, each, wide), f32),
            pltpu.VMEM((groups, deep, each, wide), f32),
            pltpu.VMEM((max(groups - 1, 1), deep, each, wide), f32),
            pltpu.VMEM((deep, each, wide), f32),
            pltpu.VMEM((max(deep - 1, 1), each, wide), f32),
            pltpu.SemaphoreType.DMA((count, chunks)),
            pltpu.SemaphoreType.DMA((count, chunks)),
        ],
        compiler_params=pltpu.CompilerParams(
            collective_id=0, has_side_effects=True, vmem_limit_bytes=48 << 20
        ),
        name="sum_grads",
    )(laid)
    return total.reshape(full, wide)[:rows, :cols]


def greet(others):
    barrier = pltpu.get_barrier_semaphore()
    for other in others:
        pl.semaphore_signal(barrier, inc=1, device_id=other, device_id_type=MESH)
    pl.semaphore_wait(barrier, len(others))


def halo_kernel(*refs):
    rows_ref, cols_ref = refs[:2]
    got_rows, got_cols = refs[2:4] if len(refs) == 6 else refs[3:5]
    send, recv = refs[-2:]
    d, w, c = (lax.axis_index(a) for a in ("dp", "row", "col"))
    count, wide = lax.axis_size("row"), lax.axis_size("col")

    def at(drow, dcol):
        return (d, lax.rem(w + drow + count, count), lax.rem(c + dcol + wide, wide))

    up, down, left, right = w > 0, w < count - 1, c > 0, c < wide - 1
    rows_there = {-1: up, 0: True, 1: down}
    cols_there = {-1: left, 0: True, 1: right}
    plan = [
        (rows_ref.at[1], got_rows.at[0], 1, 0),
        (rows_ref.at[0], got_rows.at[1], -1, 0),
    ]
    for side, dcol in enumerate((1, -1)):
        for drow in (-1, 0, 1):
            slot = got_cols.at[side * 3 + 1 - drow]
            plan.append((cols_ref.at[1 - side], slot, drow, dcol))
    layers = []
    if len(refs) > 6:
        deep = lax.axis_size("dp")
        layers = [(lax.rem(d + s, deep), w, c) for s in range(1, deep)]
    greet([at(drow, dcol) for _, _, drow, dcol in plan] + layers)

    def there(drow, dcol):
        return jnp.logical_and(rows_there[drow], cols_there[dcol])

    copies = [
        pltpu.make_async_remote_copy(
            src_ref=src,
            dst_ref=dst,
            send_sem=send.at[n],
            recv_sem=recv.at[n],
            device_id=at(drow, dcol),
            device_id_type=MESH,
        )
        for n, (src, dst, drow, dcol) in enumerate(plan)
    ]
    extra = []
    for n, to in enumerate(layers):
        copy = pltpu.make_async_remote_copy(
            src_ref=refs[2],
            dst_ref=refs[5].at[d],
            send_sem=send.at[len(plan) + n],
            recv_sem=recv.at[len(plan) + n],
            device_id=to,
            device_id_type=MESH,
        )
        extra.append(copy)
    for copy, (_, _, drow, dcol) in zip(copies, plan):
        pl.when(there(drow, dcol))(copy.start)
    for copy in extra:
        copy.start()
    if layers:
        refs[5][d] = refs[2][...]
    for copy in extra:
        copy.wait()
    for copy, (_, _, drow, dcol) in zip(copies, plan):
        pl.when(there(-drow, -dcol))(copy.wait_recv)
    for copy, (_, _, drow, dcol) in zip(copies, plan):
        pl.when(there(drow, dcol))(copy.wait_send)


def with_halo(shard, number, vectors=None):
    _, chans, rows, cols = shard.shape
    count, wide = lax.axis_size("row"), lax.axis_size("col")
    w, c = lax.axis_index("row"), lax.axis_index("col")
    own = shard[0].transpose(1, 2, 0)
    tall = -(-rows // 16) * 16
    edge_rows = jnp.stack([own[0], own[rows - 1]])
    edge_cols = jnp.stack([own[:, 0], own[:, cols - 1]])
    edge_cols = jnp.pad(edge_cols, ((0, 0), (0, tall - rows), (0, 0)))
    ins = [edge_rows, edge_cols]
    outs = [
        jax.ShapeDtypeStruct(edge_rows.shape, shard.dtype),
        jax.ShapeDtypeStruct((6, tall, chans), shard.dtype),
    ]
    copies = 8
    if vectors is not None:
        deep = lax.axis_size("dp")
        ins.append(vectors)
        outs.append(jax.ShapeDtypeStruct((deep, *vectors.shape), vectors.dtype))
        copies += deep - 1
    got_rows, got_cols, *every = pl.pallas_call(
        halo_kernel,
        out_shape=outs,
        in_specs=[pl.BlockSpec(memory_space=pltpu.VMEM)] * len(ins),
        out_specs=[pl.BlockSpec(memory_space=pltpu.VMEM)] * len(outs),
        scratch_shapes=[
            pltpu.SemaphoreType.DMA((copies,)),
            pltpu.SemaphoreType.DMA((copies,)),
        ],
        compiler_params=pltpu.CompilerParams(
            collective_id=number, has_side_effects=True, vmem_limit_bytes=48 << 20
        ),
        name="halo",
    )(*ins)
    up, down = w > 0, w < count - 1
    zero = jnp.zeros((), shard.dtype)
    above = jnp.where(up, got_rows[0], zero)[None]
    below = jnp.where(down, got_rows[1], zero)[None]

    def side(got, there):
        top = jnp.where(up, got[0, rows - 1 : rows], zero)
        bottom = jnp.where(down, got[2, 0:1], zero)
        whole = jnp.concatenate([top, got[1, :rows], bottom], axis=0)
        return jnp.where(there, whole, zero)[:, None]

    mid = jnp.concatenate([above, own, below], axis=0)
    left, right = side(got_cols[:3], c > 0), side(got_cols[3:], c < wide - 1)
    whole = jnp.concatenate([left, mid, right], axis=1).transpose(2, 0, 1)[None]
    return (whole, *every) if every else whole


def sample_kernel(v_ref, out_ref, buf, send, recv):
    d, w, c = (lax.axis_index(a) for a in ("dp", "row", "col"))
    wide = lax.axis_size("col")
    group = lax.axis_size("row") * wide
    me = w * wide + c
    others = []
    for s in range(1, group):
        at = lax.rem(me + s, group)
        others.append((d, at // wide, lax.rem(at, wide)))
    greet(others)
    copies = [
        pltpu.make_async_remote_copy(
            src_ref=v_ref,
            dst_ref=buf.at[me],
            send_sem=send.at[n],
            recv_sem=recv.at[n],
            device_id=to,
            device_id_type=MESH,
        )
        for n, to in enumerate(others)
    ]
    for copy in copies:
        copy.start()
    buf[me] = v_ref[...]
    for copy in copies:
        copy.wait()
    total = buf[0]
    for s in range(1, group):
        total = total + buf[s]
    out_ref[...] = total


def sample_sum(values):
    group = lax.axis_size("row") * lax.axis_size("col")
    return pl.pallas_call(
        sample_kernel,
        out_shape=jax.ShapeDtypeStruct(values.shape, values.dtype),
        in_specs=[pl.BlockSpec(memory_space=pltpu.VMEM)],
        out_specs=pl.BlockSpec(memory_space=pltpu.VMEM),
        scratch_shapes=[
            pltpu.VMEM((group, *values.shape), values.dtype),
            pltpu.SemaphoreType.DMA((group - 1,)),
            pltpu.SemaphoreType.DMA((group - 1,)),
        ],
        compiler_params=pltpu.CompilerParams(
            collective_id=3, has_side_effects=True, vmem_limit_bytes=48 << 20
        ),
        name="sample_sum",
    )(values)


def silu_slope(value):
    sig = jax.nn.sigmoid(value)
    return sig * (1.0 + value * (1.0 - sig))


def normalize(inputs, norm_gain):
    widened = inputs.astype(jnp.float32)
    inverse = lax.rsqrt(jnp.mean(widened * widened, axis=1, keepdims=True) + EPS)
    normed = widened * inverse
    scaled = (normed * norm_gain[None, :, None, None]).astype(jnp.bfloat16)
    return (normed, inverse, scaled)


def expand(scaled, w_expand):
    return jnp.einsum("bchw,ce->behw", scaled, w_expand, preferred_element_type=jnp.float32)


def depthwise(hidden_pad, kernel, out_rows, out_cols):
    total = jnp.zeros((hidden_pad.shape[0], hidden_pad.shape[1], out_rows, out_cols), jnp.float32)
    for tap in range(9):
        drow, dcol = (tap // 3, tap % 3)
        total = (
            total
            + kernel[:, tap][None, :, None, None]
            * hidden_pad[:, :, drow : drow + out_rows, dcol : dcol + out_cols]
        )
    return total


def local(inputs, norm_gain, w_expand, kernel, w_squeeze, w_excite, w_project, cotangent):
    batch, chans, rows, cols = inputs.shape
    pixels = rows * cols * lax.axis_size("row") * lax.axis_size("col")
    normed, inverse, scaled = normalize(inputs, norm_gain)
    pre = expand(scaled, w_expand)
    hidden = jax.nn.silu(pre).astype(jnp.bfloat16)
    hidden_pad = with_halo(hidden, 1)
    conv = depthwise(hidden_pad, kernel, rows, cols)
    act = jax.nn.silu(conv)
    grad_gated = jnp.einsum(
        "bchw,ec->behw", cotangent, w_project, preferred_element_type=jnp.float32
    )
    sums = sample_sum(
        jnp.concatenate([jnp.sum(act, axis=(2, 3)), jnp.sum(grad_gated * act, axis=(2, 3))])
    )
    pooled = sums[:batch] / pixels
    squeeze_pre = jnp.dot(pooled, w_squeeze, precision=HIGH)
    squeezed = jax.nn.silu(squeeze_pre)
    excite_pre = jnp.dot(squeezed, w_excite, precision=HIGH)
    excite = jax.nn.sigmoid(excite_pre)
    gated = (act * excite[:, :, None, None]).astype(jnp.bfloat16)
    proj = jnp.einsum("behw,ec->bchw", gated, w_project, preferred_element_type=jnp.float32)
    output = (inputs.astype(jnp.float32) + proj).astype(jnp.bfloat16)
    grad_project = jnp.einsum("bchw,behw->ce", cotangent, gated, preferred_element_type=jnp.float32)
    grad_excite = sums[batch:]
    grad_epre = grad_excite * excite * (1.0 - excite)
    grad_spre = jnp.einsum("be,se->bs", grad_epre, w_excite, precision=HIGH) * silu_slope(
        squeeze_pre
    )
    grad_pooled = jnp.einsum("bs,es->be", grad_spre, w_squeeze, precision=HIGH)
    grad_act = grad_gated * excite[:, :, None, None] + (grad_pooled / pixels)[:, :, None, None]
    grad_conv = (grad_act * silu_slope(conv)).astype(jnp.bfloat16)
    spare = ((0, 0), (0, pooled.shape[1] - squeezed.shape[1]))
    vectors = [pooled, grad_epre, jnp.pad(squeezed, spare), jnp.pad(grad_spre, spare)]
    grad_pad, every = with_halo(grad_conv, 2, jnp.concatenate(vectors))
    every = every.reshape(-1, 4, *pooled.shape)
    all_pooled, all_epre = every[:, 0], every[:, 1]
    all_squeezed, all_spre = (every[:, n, :, : squeezed.shape[1]] for n in (2, 3))
    grad_wsq_all = jnp.einsum("dbs,dbe->se", all_spre, all_pooled, precision=HIGH).T
    grad_wexc_all = jnp.einsum("dbs,dbe->se", all_squeezed, all_epre, precision=HIGH)
    grad_hidden = jnp.zeros(pre.shape, jnp.float32)
    taps = []
    for tap in range(9):
        drow, dcol = (tap // 3, tap % 3)
        grad_hidden = (
            grad_hidden
            + kernel[:, tap][None, :, None, None]
            * grad_pad[:, :, 2 - drow : 2 - drow + rows, 2 - dcol : 2 - dcol + cols]
        )
        taps.append(
            jnp.sum(
                grad_conv.astype(jnp.float32)
                * hidden_pad[:, :, drow : drow + rows, dcol : dcol + cols].astype(jnp.float32),
                axis=(0, 2, 3),
            )
        )
    grad_kernel = jnp.stack(taps, axis=0)
    grad_pre = (grad_hidden * silu_slope(pre)).astype(jnp.bfloat16)
    grad_wexp = jnp.einsum("bchw,behw->ce", scaled, grad_pre, preferred_element_type=jnp.float32)
    grad_scaled = jnp.einsum(
        "ce,behw->bchw", w_expand, grad_pre, preferred_element_type=jnp.float32
    )
    grad_gain = jnp.sum(grad_scaled * normed, axis=(0, 2, 3))
    grad_normed = grad_scaled * norm_gain[None, :, None, None]
    grad_in = inverse * (
        grad_normed - normed * jnp.mean(grad_normed * normed, axis=1, keepdims=True)
    ) + cotangent.astype(jnp.float32)
    hidden_n = grad_project.shape[1]
    pieces = [
        grad_project,
        grad_wexp,
        grad_kernel,
        jnp.pad(grad_gain, (0, hidden_n - chans))[None],
    ]
    sizes = [p.shape[0] for p in pieces]
    height, width = sum(sizes), chunk_of(hidden_n)
    starts = range(0, hidden_n, width)
    total = sum_all(jnp.concatenate([p[:, k : k + width] for k in starts for p in pieces], axis=0))
    ends = [sum(sizes[: n + 1]) for n in range(len(sizes))]
    parts = [
        jnp.concatenate(
            [total[k * height + e - n : k * height + e] for k in range(len(starts))], axis=1
        )
        for e, n in zip(ends, sizes)
    ]
    project_all, wexp_all, kernel_all = parts[0].T, parts[1], parts[2].T
    gain_all = parts[3][0, :chans]
    return (
        output,
        grad_in.astype(jnp.bfloat16),
        gain_all,
        wexp_all,
        kernel_all,
        grad_wsq_all,
        grad_wexc_all,
        project_all,
    )


def solution(mesh):
    placed = (
        P("dp", None, "row", "col"),
        P(),
        P(),
        P(),
        P(),
        P(),
        P(),
        P("dp", None, "row", "col"),
    )
    return jax.shard_map(
        local,
        mesh=mesh,
        in_specs=placed,
        out_specs=(
            P("dp", None, "row", "col"),
            P("dp", None, "row", "col"),
            P(),
            P(),
            P(),
            P(),
            P(),
            P(),
        ),
        check_vma=False,
    )
```

```python
import jax
import jax.numpy as jnp
from jax import lax
from jax.experimental import pallas as pl
from jax.experimental.pallas import tpu as pltpu
from jax.sharding import PartitionSpec as P

EPS = 1e-06
HIGH = lax.Precision.HIGHEST

MESH = pl.DeviceIdType.MESH

def sum_kernel(v_ref, out_ref, mate_buf, acc1, group_buf, acc2, deep_buf, send, recv):
    groups, deep = v_ref.shape[1], v_ref.shape[2]
    half_cols = lax.axis_size("col") // 2
    d, w, c = (lax.axis_index(a) for a in ("dp", "row", "col"))
    core = lax.rem(c, 2)
    g = w * half_cols + c // 2

    def mate():
        return (d, w, c + 1 - 2 * core)

    def peer(s):
        at = lax.rem(g + s, groups)
        return at, (d, at // half_cols, lax.rem(at, half_cols) * 2 + core)

    def layer(s):
        at = lax.rem(d + s, deep)
        return at, (at, w, c)

    barrier = pltpu.get_barrier_semaphore()
    others = [mate()] + [peer(s)[1] for s in range(1, groups)]
    others += [layer(s)[1] for s in range(1, deep)]
    for other in others:
        pl.semaphore_signal(barrier, inc=1, device_id=other, device_id_type=MESH)
    pl.semaphore_wait(barrier, len(others))

    width = chunk_of(v_ref.shape[-1])
    chunks = range(v_ref.shape[-1] // width)
    sent = []

    def go(src, dst, n, k, to):
        copy = pltpu.make_async_remote_copy(
            src_ref=src,
            dst_ref=dst,
            send_sem=send.at[n, k],
            recv_sem=recv.at[n, k],
            device_id=to,
            device_id_type=MESH,
        )
        copy.start()
        sent.append(copy)
        return copy

    cuts = [pl.ds(k * width, width) for k in chunks]
    arriving = []
    for k in chunks:
        src = v_ref.at[1 - core, :, :, :, cuts[k]]
        arriving.append([go(src, mate_buf.at[:, :, :, cuts[k]], 0, k, mate())])

    def landed(k):
        for copy in arriving[k]:
            copy.wait_recv()
        arriving[k] = []

    for k in chunks:
        landed(k)
        cut = cuts[k]
        acc1[:, :, :, cut] = v_ref[core, :, :, :, cut] + mate_buf[:, :, :, cut]
        for s in range(1, groups):
            at, to = peer(s)
            src, dst = acc1.at[at, :, :, cut], group_buf.at[s - 1, :, :, cut]
            arriving[k].append(go(src, dst, s, k, to))
    n = groups - 1
    for k in chunks:
        landed(k)
        cut = cuts[k]
        part = acc1[g, :, :, cut]
        for s in range(1, groups):
            part = part + group_buf[s - 1, :, :, cut]
        acc2[:, :, cut] = part
        for s in range(1, deep):
            at, to = layer(s)
            src, dst = acc2.at[at, :, cut], deep_buf.at[s - 1, :, cut]
            arriving[k].append(go(src, dst, n + s, k, to))
    n += deep - 1
    for k in chunks:
        landed(k)
        cut = cuts[k]
        part = acc2[d, :, cut]
        for s in range(1, deep):
            part = part + deep_buf[s - 1, :, cut]
        out_ref[core, g, d, :, cut] = part
        mine = out_ref.at[core, g, d, :, cut]
        for s in range(1, deep):
            arriving[k].append(go(mine, mine, n + s, k, layer(s)[1]))
    n += deep - 1
    for k in chunks:
        landed(k)
        mine = out_ref.at[core, g, :, :, cuts[k]]
        for s in range(1, groups):
            arriving[k].append(go(mine, mine, n + s, k, peer(s)[1]))
    n += groups
    for k in chunks:
        landed(k)
        mine = out_ref.at[core, :, :, :, cuts[k]]
        arriving[k].append(go(mine, mine, n, k, mate()))
    for k in chunks:
        landed(k)
    for copy in sent:
        copy.wait_send()


def chunk_of(wide):
    return 128 if wide % 128 == 0 else wide


def sum_all(values):
    rows, cols = values.shape
    groups = lax.axis_size("row") * (lax.axis_size("col") // 2)
    deep = lax.axis_size("dp")
    each = -(-rows // (2 * groups * deep))
    wide = -(-cols // 128) * 128
    full = 2 * groups * deep * each
    laid = jnp.pad(values, ((0, full - rows), (0, wide - cols)))
    laid = laid.reshape(2, groups, deep, each, wide)
    f32 = jnp.float32
    count = 2 * (1 + groups - 1 + deep - 1) + 1
    total = pl.pallas_call(
        sum_kernel,
        out_shape=jax.ShapeDtypeStruct(laid.shape, f32),
        in_specs=[pl.BlockSpec(memory_space=pltpu.VMEM)],
        out_specs=pl.BlockSpec(memory_space=pltpu.VMEM),
        scratch_shapes=[
            pltpu.VMEM((groups, deep, each, wide), f32),
            pltpu.VMEM((groups, deep, each, wide), f32),
            pltpu.VMEM((max(groups - 1, 1), deep, each, wide), f32),
            pltpu.VMEM((deep, each, wide), f32),
            pltpu.VMEM((max(deep - 1, 1), each, wide), f32),
            pltpu.SemaphoreType.DMA((count, wide // chunk_of(wide))),
            pltpu.SemaphoreType.DMA((count, wide // chunk_of(wide))),
        ],
        compiler_params=pltpu.CompilerParams(
            collective_id=0, has_side_effects=True, vmem_limit_bytes=48 << 20
        ),
        name="sum_grads",
    )(laid)
    return total.reshape(full, wide)[:rows, :cols]


def greet(others):
    barrier = pltpu.get_barrier_semaphore()
    for other in others:
        pl.semaphore_signal(barrier, inc=1, device_id=other, device_id_type=MESH)
    pl.semaphore_wait(barrier, len(others))


def halo_kernel(rows_ref, cols_ref, got_rows, got_cols, send, recv):
    d, w, c = (lax.axis_index(a) for a in ("dp", "row", "col"))
    count, wide = lax.axis_size("row"), lax.axis_size("col")

    def at(drow, dcol):
        return (d, lax.rem(w + drow + count, count), lax.rem(c + dcol + wide, wide))

    up, down, left, right = w > 0, w < count - 1, c > 0, c < wide - 1
    rows_there = {-1: up, 0: True, 1: down}
    cols_there = {-1: left, 0: True, 1: right}
    plan = [
        (rows_ref.at[1], got_rows.at[0], 1, 0),
        (rows_ref.at[0], got_rows.at[1], -1, 0),
    ]
    for side, dcol in enumerate((1, -1)):
        for drow in (-1, 0, 1):
            slot = got_cols.at[side * 3 + 1 - drow]
            plan.append((cols_ref.at[1 - side], slot, drow, dcol))
    greet([at(drow, dcol) for _, _, drow, dcol in plan])

    def there(drow, dcol):
        return jnp.logical_and(rows_there[drow], cols_there[dcol])

    copies = [
        pltpu.make_async_remote_copy(
            src_ref=src,
            dst_ref=dst,
            send_sem=send.at[n],
            recv_sem=recv.at[n],
            device_id=at(drow, dcol),
            device_id_type=MESH,
        )
        for n, (src, dst, drow, dcol) in enumerate(plan)
    ]
    for copy, (_, _, drow, dcol) in zip(copies, plan):
        pl.when(there(drow, dcol))(copy.start)
    for copy, (_, _, drow, dcol) in zip(copies, plan):
        pl.when(there(-drow, -dcol))(copy.wait_recv)
    for copy, (_, _, drow, dcol) in zip(copies, plan):
        pl.when(there(drow, dcol))(copy.wait_send)


def with_halo(shard, number):
    _, chans, rows, cols = shard.shape
    count, wide = lax.axis_size("row"), lax.axis_size("col")
    w, c = lax.axis_index("row"), lax.axis_index("col")
    own = shard[0].transpose(1, 2, 0)
    tall = -(-rows // 16) * 16
    edge_rows = jnp.stack([own[0], own[rows - 1]])
    edge_cols = jnp.stack([own[:, 0], own[:, cols - 1]])
    edge_cols = jnp.pad(edge_cols, ((0, 0), (0, tall - rows), (0, 0)))
    got_rows, got_cols = pl.pallas_call(
        halo_kernel,
        out_shape=[
            jax.ShapeDtypeStruct(edge_rows.shape, shard.dtype),
            jax.ShapeDtypeStruct((6, tall, chans), shard.dtype),
        ],
        in_specs=[pl.BlockSpec(memory_space=pltpu.VMEM)] * 2,
        out_specs=[pl.BlockSpec(memory_space=pltpu.VMEM)] * 2,
        scratch_shapes=[pltpu.SemaphoreType.DMA((8,)), pltpu.SemaphoreType.DMA((8,))],
        compiler_params=pltpu.CompilerParams(
            collective_id=number, has_side_effects=True, vmem_limit_bytes=48 << 20
        ),
        name="halo",
    )(edge_rows, edge_cols)
    up, down = w > 0, w < count - 1
    zero = jnp.zeros((), shard.dtype)
    above = jnp.where(up, got_rows[0], zero)[None]
    below = jnp.where(down, got_rows[1], zero)[None]

    def side(got, there):
        top = jnp.where(up, got[0, rows - 1 : rows], zero)
        bottom = jnp.where(down, got[2, 0:1], zero)
        whole = jnp.concatenate([top, got[1, :rows], bottom], axis=0)
        return jnp.where(there, whole, zero)[:, None]

    mid = jnp.concatenate([above, own, below], axis=0)
    left, right = side(got_cols[:3], c > 0), side(got_cols[3:], c < wide - 1)
    return jnp.concatenate([left, mid, right], axis=1).transpose(2, 0, 1)[None]


def sample_kernel(v_ref, out_ref, buf, send, recv):
    d, w, c = (lax.axis_index(a) for a in ("dp", "row", "col"))
    wide = lax.axis_size("col")
    group = lax.axis_size("row") * wide
    me = w * wide + c
    others = []
    for s in range(1, group):
        at = lax.rem(me + s, group)
        others.append((d, at // wide, lax.rem(at, wide)))
    greet(others)
    copies = [
        pltpu.make_async_remote_copy(
            src_ref=v_ref,
            dst_ref=buf.at[me],
            send_sem=send.at[n],
            recv_sem=recv.at[n],
            device_id=to,
            device_id_type=MESH,
        )
        for n, to in enumerate(others)
    ]
    for copy in copies:
        copy.start()
    buf[me] = v_ref[...]
    for copy in copies:
        copy.wait()
    total = buf[0]
    for s in range(1, group):
        total = total + buf[s]
    out_ref[...] = total


def sample_sum(values):
    group = lax.axis_size("row") * lax.axis_size("col")
    return pl.pallas_call(
        sample_kernel,
        out_shape=jax.ShapeDtypeStruct(values.shape, values.dtype),
        in_specs=[pl.BlockSpec(memory_space=pltpu.VMEM)],
        out_specs=pl.BlockSpec(memory_space=pltpu.VMEM),
        scratch_shapes=[
            pltpu.VMEM((group, *values.shape), values.dtype),
            pltpu.SemaphoreType.DMA((group - 1,)),
            pltpu.SemaphoreType.DMA((group - 1,)),
        ],
        compiler_params=pltpu.CompilerParams(
            collective_id=3, has_side_effects=True, vmem_limit_bytes=48 << 20
        ),
        name="sample_sum",
    )(values)


def silu_slope(value):
    sig = jax.nn.sigmoid(value)
    return sig * (1.0 + value * (1.0 - sig))


def normalize(inputs, norm_gain):
    widened = inputs.astype(jnp.float32)
    inverse = lax.rsqrt(jnp.mean(widened * widened, axis=1, keepdims=True) + EPS)
    normed = widened * inverse
    scaled = (normed * norm_gain[None, :, None, None]).astype(jnp.bfloat16)
    return (normed, inverse, scaled)


def expand(scaled, w_expand):
    return jnp.einsum("bchw,ce->behw", scaled, w_expand, preferred_element_type=jnp.float32)


def depthwise(hidden_pad, kernel, out_rows, out_cols):
    total = jnp.zeros((hidden_pad.shape[0], hidden_pad.shape[1], out_rows, out_cols), jnp.float32)
    for tap in range(9):
        drow, dcol = (tap // 3, tap % 3)
        total = (
            total
            + kernel[:, tap][None, :, None, None]
            * hidden_pad[:, :, drow : drow + out_rows, dcol : dcol + out_cols]
        )
    return total


def local(inputs, norm_gain, w_expand, kernel, w_squeeze, w_excite, w_project, cotangent):
    batch, chans, rows, cols = inputs.shape
    pixels = rows * cols * lax.axis_size("row") * lax.axis_size("col")
    normed, inverse, scaled = normalize(inputs, norm_gain)
    pre = expand(scaled, w_expand)
    hidden = jax.nn.silu(pre).astype(jnp.bfloat16)
    hidden_pad = with_halo(hidden, 1)
    conv = depthwise(hidden_pad, kernel, rows, cols)
    act = jax.nn.silu(conv)
    grad_gated = jnp.einsum(
        "bchw,ec->behw", cotangent, w_project, preferred_element_type=jnp.float32
    )
    sums = sample_sum(
        jnp.concatenate([jnp.sum(act, axis=(2, 3)), jnp.sum(grad_gated * act, axis=(2, 3))])
    )
    pooled = sums[:batch] / pixels
    squeeze_pre = jnp.dot(pooled, w_squeeze, precision=HIGH)
    squeezed = jax.nn.silu(squeeze_pre)
    excite_pre = jnp.dot(squeezed, w_excite, precision=HIGH)
    excite = jax.nn.sigmoid(excite_pre)
    gated = (act * excite[:, :, None, None]).astype(jnp.bfloat16)
    proj = jnp.einsum("behw,ec->bchw", gated, w_project, preferred_element_type=jnp.float32)
    output = (inputs.astype(jnp.float32) + proj).astype(jnp.bfloat16)
    grad_project = jnp.einsum("bchw,behw->ce", cotangent, gated, preferred_element_type=jnp.float32)
    grad_excite = sums[batch:]
    grad_epre = grad_excite * excite * (1.0 - excite)
    grad_wexc = jnp.einsum("bs,be->se", squeezed, grad_epre, precision=HIGH)
    grad_spre = jnp.einsum("be,se->bs", grad_epre, w_excite, precision=HIGH) * silu_slope(
        squeeze_pre
    )
    grad_wsq = jnp.einsum("bs,be->se", grad_spre, pooled, precision=HIGH)
    grad_pooled = jnp.einsum("bs,es->be", grad_spre, w_squeeze, precision=HIGH)
    grad_act = grad_gated * excite[:, :, None, None] + (grad_pooled / pixels)[:, :, None, None]
    grad_conv = (grad_act * silu_slope(conv)).astype(jnp.bfloat16)
    grad_pad = with_halo(grad_conv, 2)
    grad_hidden = jnp.zeros(pre.shape, jnp.float32)
    taps = []
    for tap in range(9):
        drow, dcol = (tap // 3, tap % 3)
        grad_hidden = (
            grad_hidden
            + kernel[:, tap][None, :, None, None]
            * grad_pad[:, :, 2 - drow : 2 - drow + rows, 2 - dcol : 2 - dcol + cols]
        )
        taps.append(
            jnp.sum(
                grad_conv.astype(jnp.float32)
                * hidden_pad[:, :, drow : drow + rows, dcol : dcol + cols].astype(jnp.float32),
                axis=(0, 2, 3),
            )
        )
    grad_kernel = jnp.stack(taps, axis=0)
    grad_pre = (grad_hidden * silu_slope(pre)).astype(jnp.bfloat16)
    grad_wexp = jnp.einsum("bchw,behw->ce", scaled, grad_pre, preferred_element_type=jnp.float32)
    grad_scaled = jnp.einsum(
        "ce,behw->bchw", w_expand, grad_pre, preferred_element_type=jnp.float32
    )
    grad_gain = jnp.sum(grad_scaled * normed, axis=(0, 2, 3))
    grad_normed = grad_scaled * norm_gain[None, :, None, None]
    grad_in = inverse * (
        grad_normed - normed * jnp.mean(grad_normed * normed, axis=1, keepdims=True)
    ) + cotangent.astype(jnp.float32)
    lead = jnp.logical_and(lax.axis_index("row") == 0, lax.axis_index("col") == 0)
    keep = lead.astype(jnp.float32)
    hidden_n = grad_project.shape[1]
    pieces = [
        grad_project,
        grad_wexp,
        grad_kernel,
        grad_wsq * keep,
        grad_wexc * keep,
        jnp.pad(grad_gain, (0, hidden_n - chans))[None],
    ]
    sizes = [p.shape[0] for p in pieces]
    total = sum_all(jnp.concatenate(pieces, axis=0))
    ends = [sum(sizes[: n + 1]) for n in range(len(sizes))]
    parts = [total[e - n : e] for e, n in zip(ends, sizes)]
    project_all, wexp_all, kernel_all = parts[0].T, parts[1], parts[2].T
    grad_wsq_all, grad_wexc_all, gain_all = parts[3].T, parts[4], parts[5][0, :chans]
    return (
        output,
        grad_in.astype(jnp.bfloat16),
        gain_all,
        wexp_all,
        kernel_all,
        grad_wsq_all,
        grad_wexc_all,
        project_all,
    )


def solution(mesh):
    placed = (
        P("dp", None, "row", "col"),
        P(),
        P(),
        P(),
        P(),
        P(),
        P(),
        P("dp", None, "row", "col"),
    )
    return jax.shard_map(
        local,
        mesh=mesh,
        in_specs=placed,
        out_specs=(
            P("dp", None, "row", "col"),
            P("dp", None, "row", "col"),
            P(),
            P(),
            P(),
            P(),
            P(),
            P(),
        ),
        check_vma=False,
    )
```
